128 devices in a mesh: row: 8 (over y_lo, z), col: 16 (over x, y_hi, core).
Axes of the slice: x: 4, y: 4 (y_hi: 2, y_lo: 2; y = y_hi * 2 + y_lo), z: 4, core: 2. Of those that a mesh axis runs over, the one named last changes fastest.
Arguments:
- amplitudes: float32 [2, 4096, 2048], P(None, 'row', 'col'), may hold values from -6 to 6
- integrals: float32 [2, 1024, 128, 128], P(None, 'col'), may hold values from -0.1875 to 0.1875
- tile_rows: int32 [2, 1024], replicated, may hold values from 0 to 15
- tile_reader: int32 [2, 1024, 1], replicated, may hold values from 0 to 15, as said below
- tile_column: int32 [2, 1024], replicated, may hold values from 0 to 15
Outputs:
- ladder: float32 [4096, 32768], P('row', 'col')
The draws below stay inside these ranges and needn't reach their ends.
Inputs may be any that keep to these rules, and one draw needn't show every extreme that they name: `tile_reader`: rows of one panel fall in aligned blocks of 64, one block for the tiles held by one index of col. For each panel and reader column, exactly 64 held tiles name it, and their pairs (tile_rows, tile_column) are all different. Within a block no reader column is named more than 8 times, and in every panel every block names some reader column exactly 8 times.
All inputs are finite; a program needn't handle non-finite values.
Results may differ from the reference program's by a relative error of at most 0.0001.
Values sent between devices are 32-bit elements; how exact they have to be, the bound alone decides.
No kernel may reach another device: no remote copies, remote signals or barrier semaphores. Data moves between devices by JAX's collectives and lax.ppermute only.
A program may use at most 192 MiB of HBM per device.

```python
import jax
import jax.numpy as jnp
from jax import lax

TILE = 128
STEPS = 2
NT_DEV = 16
H_PAIR = 4
P_SIZE = 4096
KT = 16
NT = 256
HOLD = 64
N_COL = 16


def screen_layout(key):
    cell_count = KT * NT_DEV

    def one_panel(panel_key):
        perm_key, shift_key, order_key = jax.random.split(panel_key, 3)
        reader_keys = jax.random.split(perm_key, N_COL)
        chosen_cells = jax.vmap(lambda kk: jax.random.permutation(kk, cell_count).astype(jnp.int32))(reader_keys)
        shift = jax.random.randint(shift_key, (), 0, N_COL, dtype=jnp.int32)
        holder_ids = jnp.arange(N_COL, dtype=jnp.int32)[:, None]
        reader_ids = jnp.arange(N_COL, dtype=jnp.int32)[None, :]
        distance = (reader_ids - holder_ids - shift) % N_COL
        counts = jnp.where(distance == 0, 2 * H_PAIR, jnp.where(distance == 1, 0, H_PAIR)).astype(jnp.int32)
        reader_start = (jnp.cumsum(counts, axis=0) - counts).astype(jnp.int32)
        holder_end = jnp.cumsum(counts, axis=1).astype(jnp.int32)
        holder_begin = holder_end - counts
        positions = jnp.arange(HOLD, dtype=jnp.int32)
        reader_of = jnp.sum((positions[None, :, None] >= holder_end[:, None, :]).astype(jnp.int32), axis=2).astype(jnp.int32)
        offset = positions[None, :] - jnp.take_along_axis(holder_begin, reader_of, axis=1)
        place = jnp.take_along_axis(reader_start, reader_of, axis=1) + offset
        cell_of = chosen_cells[reader_of, place]
        order_keys = jax.random.split(order_key, N_COL)
        orders = jax.vmap(lambda kk: jax.random.permutation(kk, HOLD).astype(jnp.int32))(order_keys)
        reader_of = jnp.take_along_axis(reader_of, orders, axis=1)
        cell_of = jnp.take_along_axis(cell_of, orders, axis=1)
        return (reader_of.reshape(-1), cell_of.reshape(-1))
    readers, cells = jax.vmap(one_panel)(jax.random.split(key, STEPS))
    return (readers.astype(jnp.int32), (cells // NT_DEV).astype(jnp.int32), (cells % NT_DEV).astype(jnp.int32))


def draw_tile_rows(key, part):
    readers, rows_drawn, columns_drawn = screen_layout(key)
    return rows_drawn


def draw_tile_reader(key, part):
    readers, rows_drawn, columns_drawn = screen_layout(key)
    return readers[:, :, None]


def draw_tile_column(key, part):
    readers, rows_drawn, columns_drawn = screen_layout(key)
    return columns_drawn


def level_of(stream_key, shape, cuts, low, largest):
    gain, own = 1.0, jax.random.fold_in(stream_key, 6)
    for axis_at, shards_of in cuts:
        steps = jnp.exp(jax.random.uniform(jax.random.fold_in(own, axis_at), (shards_of,), jnp.float32, low / len(cuts), largest / len(cuts)))
        gain = gain * jnp.repeat(steps, shape[axis_at] // shards_of).reshape([-1 if axis == axis_at else 1 for axis in range(len(shape))])
    return gain


def centred(rng, dims, deviation, most, cuts=(), held_as=jnp.bfloat16):
    drawn = deviation * jax.random.normal(rng, dims, jnp.float32)
    if cuts:
        drawn = drawn * level_of(rng, dims, cuts, -0.22, 0.18)
    return jnp.clip(drawn, -most, most).astype(held_as)


def setup_inputs(seed: int = 0) -> dict:
    arg_keys = jax.random.split(jax.random.key(seed), 6)
    return {
        "amplitudes": centred(arg_keys[0], (STEPS, P_SIZE, KT * TILE), 1.0, 6.0, ((1, 8), (2, 16)), jnp.float32),
        "integrals": centred(arg_keys[1], (STEPS, N_COL * HOLD, TILE, TILE), (TILE * STEPS * KT // 4) ** -0.5, 0.1875, ((1, 16),), jnp.float32),
        "tile_rows": draw_tile_rows(jax.random.fold_in(arg_keys[5], 71), 0),
        "tile_reader": draw_tile_reader(jax.random.fold_in(arg_keys[5], 71), 0),
        "tile_column": draw_tile_column(jax.random.fold_in(arg_keys[5], 71), 0),
    }


def reference(amplitudes, integrals, tile_rows, tile_reader, tile_column):
    ladder = jnp.zeros((P_SIZE, NT, TILE), jnp.float32)
    for step_index in range(STEPS):
        amp_panel = amplitudes[step_index].reshape(P_SIZE, KT, TILE)
        row_tiles = tile_rows[step_index].reshape(N_COL, HOLD)
        col_tiles = (tile_reader[step_index, :, 0] * NT_DEV + tile_column[step_index]).reshape(N_COL, HOLD)
        tile_blocks = integrals[step_index].reshape(N_COL, HOLD, TILE, TILE)

        def one_holder(running, entries):
            holder_rows, holder_cols, holder_blocks = entries
            chosen = jnp.take(amp_panel, holder_rows, axis=1)
            contrib = jnp.einsum("phk,hkn->phn", chosen, holder_blocks, precision=lax.Precision.HIGHEST)
            return running.at[:, holder_cols, :].add(contrib), None

        ladder, _ = lax.scan(one_holder, ladder, (row_tiles, col_tiles, tile_blocks))
    return ladder.reshape(P_SIZE, NT * TILE)
```

```python
import functools

import jax
import jax.numpy as jnp
from jax import lax
from jax.experimental import pallas as pl
from jax.experimental.pallas import tpu as pltpu
from jax.sharding import PartitionSpec as P

TILE = 128
STEPS = 2
NT_DEV = 16
N_COL = 16
N_ROW = 8
Z = 4
HOLD = 64
CHUNK = HOLD // N_ROW
LANES = 128
VMEM_LIMIT = 56 * 1024 * 1024


def route_kernel(reader_ref, row_ref, column_ref, tiles_ref, meta_ref, *rest):
    out_ref, meta_smem, meta_sem, sems = rest
    me_row = lax.axis_index("row")
    me_col = lax.axis_index("col")
    groups = reader_ref.shape[1]
    lane = lax.broadcasted_iota(jnp.int32, (1, LANES), 1)
    upto = (
        lax.broadcasted_iota(jnp.int32, (LANES, LANES), 0)
        <= lax.broadcasted_iota(jnp.int32, (LANES, LANES), 1)
    ).astype(jnp.bfloat16)
    names = lax.broadcasted_iota(jnp.int32, (N_COL, LANES), 0)
    numbers = lax.broadcasted_iota(jnp.int32, (HOLD, LANES), 0)
    ones = jnp.ones((8, LANES), jnp.bfloat16)

    def to_lanes(sums):
        return lax.dot_general(
            ones, sums.astype(jnp.bfloat16), (((1,), (1,)), ((), ())), preferred_element_type=jnp.float32
        )

    for s in range(STEPS):
        readers = reader_ref[s]
        named = [(readers[g : g + 1] == names) for g in range(groups)]
        onehot = jnp.concatenate([n.astype(jnp.bfloat16) for n in named], axis=0)
        within = jnp.dot(onehot, upto, preferred_element_type=jnp.float32)
        before = jnp.zeros((N_COL, 1), jnp.float32)
        send = jnp.zeros((N_COL, LANES), jnp.float32)
        code = jnp.zeros((HOLD, LANES), jnp.float32)
        holder = jnp.zeros((HOLD, LANES), jnp.float32)
        for g in range(groups):
            count = within[g * N_COL : (g + 1) * N_COL]
            number = (count + before - 1.0).astype(jnp.int32)
            before = before + count[:, LANES - 1 :]
            held = lane + g * LANES
            sent = named[g] & (held // HOLD == me_col) & (number % N_ROW == me_row)
            send = send + jnp.where(sent, (held % HOLD).astype(jnp.float32), 0.0)
            place = jnp.sum(jnp.where(named[g], number, 0), axis=0, keepdims=True)
            mine = (place == numbers) & (readers[g : g + 1] == me_col)
            tile_code = row_ref[s, g : g + 1] * NT_DEV + column_ref[s, g : g + 1]
            code = code + jnp.where(mine, tile_code.astype(jnp.float32), 0.0)
            holder = holder + jnp.where(mine, (held // HOLD).astype(jnp.float32), 0.0)
        parts = [to_lanes(code)[:1], to_lanes(holder)[:1], to_lanes(send)[:1]]
        for at, part in enumerate(parts):
            meta_ref[s * 8 + at : s * 8 + at + 1, : part.shape[1]] = part.astype(jnp.int32)
    copy = pltpu.make_async_copy(meta_ref, meta_smem, meta_sem)
    copy.start()
    copy.wait()
    copies = []
    for s in range(STEPS):
        for r in range(N_COL):
            tile = meta_smem[s * 8 + 2, r]
            copies.append(
                pltpu.make_async_copy(tiles_ref.at[s, tile], out_ref.at[r, s], sems.at[len(copies)])
            )
            copies[-1].start()
    for copy in copies:
        copy.wait()


def route(readers, rows, columns, tiles):
    vmem = pl.BlockSpec(memory_space=pltpu.VMEM)
    return pl.pallas_call(
        route_kernel,
        out_shape=(
            jax.ShapeDtypeStruct((8 * STEPS, LANES), jnp.int32),
            jax.ShapeDtypeStruct((N_COL, STEPS, TILE, TILE), jnp.float32),
        ),
        in_specs=[vmem, vmem, vmem, pl.BlockSpec(memory_space=pltpu.HBM)],
        out_specs=(vmem, vmem),
        scratch_shapes=[
            pltpu.SMEM((8 * STEPS, LANES), jnp.int32),
            pltpu.SemaphoreType.DMA,
            pltpu.SemaphoreType.DMA((STEPS * N_COL,)),
        ],
        name="route",
    )(readers, rows, columns, tiles)


def compact_kernel(passed, meta_ref, arrived_ref, *rest):
    out_ref, sems = rest[-2 - passed], rest[-1]
    me_row = lax.axis_index("row")
    copies = []
    for s in range(STEPS):
        for j in range(CHUNK):
            holder = meta_ref[s * 8 + 1, j * N_ROW + me_row]
            at = len(copies)
            copies.append(pltpu.make_async_copy(arrived_ref.at[holder, s], out_ref.at[at], sems.at[at]))
            copies[-1].start()
    for copy in copies:
        copy.wait()


def compact(meta, arrived, passed):
    tiles = STEPS * CHUNK
    hbm = pl.BlockSpec(memory_space=pltpu.HBM)
    return pl.pallas_call(
        functools.partial(compact_kernel, len(passed)),
        out_shape=[jax.ShapeDtypeStruct((tiles, TILE, TILE), jnp.float32)]
        + [jax.ShapeDtypeStruct(p.shape, p.dtype) for p in passed],
        grid_spec=pltpu.PrefetchScalarGridSpec(
            num_scalar_prefetch=1,
            grid=(1,),
            in_specs=[hbm] * (1 + len(passed)),
            out_specs=[pl.BlockSpec((tiles, TILE, TILE), lambda n, meta: (0, 0, 0))] + [hbm] * len(passed),
            scratch_shapes=[pltpu.SemaphoreType.DMA((tiles,))],
        ),
        input_output_aliases={2 + n: 1 + n for n in range(len(passed))},
        name="compact",
    )(meta, arrived, *passed)


def regroup_kernel(plan, passed, *refs):
    outs, sems = refs[-1 - passed - len(plan) : -1 - passed], refs[-1]
    copies = []
    for out, parts in zip(outs, plan):
        begin = 0
        for source, first, size in parts:
            copies.append(
                pltpu.make_async_copy(
                    refs[source].at[pl.ds(first, size)], out.at[pl.ds(begin, size)], sems.at[len(copies)]
                )
            )
            copies[-1].start()
            begin += size
    for copy in copies:
        copy.wait()


def regroup(chunks, plan, passed=(), earlier=()):
    any_space, hbm = pl.BlockSpec(memory_space=pl.ANY), pl.BlockSpec(memory_space=pltpu.HBM)
    shapes = [(sum(size for _, _, size in parts),) + chunks[0].shape[1:] for parts in plan]
    before = len(chunks) + len(earlier)
    return pl.pallas_call(
        functools.partial(regroup_kernel, plan, len(passed)),
        out_shape=[jax.ShapeDtypeStruct(shape, jnp.float32) for shape in shapes]
        + [jax.ShapeDtypeStruct(p.shape, p.dtype) for p in passed],
        in_specs=[any_space] * before + [hbm] * len(passed),
        out_specs=[pl.BlockSpec(memory_space=pltpu.VMEM)] * len(plan) + [hbm] * len(passed),
        scratch_shapes=[pltpu.SemaphoreType.DMA((sum(len(parts) for parts in plan),))],
        input_output_aliases={before + n: len(plan) + n for n in range(len(passed))},
        compiler_params=pltpu.CompilerParams(vmem_limit_bytes=VMEM_LIMIT),
        name="regroup",
    )(*chunks, *earlier, *passed)


def split_kernel(*refs):
    out_ref = refs[-1]
    for at, ref in enumerate(refs[:-1]):
        value = ref[0]
        high = value.astype(jnp.bfloat16)
        out_ref[at // 8, at // 4 % 2, at % 4, 0, :, :TILE] = high
        out_ref[at // 8, at // 4 % 2, at % 4, 0, :, TILE:] = (value - high.astype(jnp.float32)).astype(jnp.bfloat16)


def split_amplitudes(pieces):
    panels, rows = pieces[0].shape[:2]
    return pl.pallas_call(
        split_kernel,
        out_shape=jax.ShapeDtypeStruct((2, 2, 4, panels, rows, 2 * TILE), jnp.bfloat16),
        grid=(panels, 2),
        in_specs=[pl.BlockSpec((1, rows // 2, TILE), lambda s, n: (s, n, 0))] * 16,
        out_specs=pl.BlockSpec((2, 2, 4, 1, rows // 2, 2 * TILE), lambda s, n: (0, 0, 0, s, n, 0)),
        compiler_params=pltpu.CompilerParams(vmem_limit_bytes=VMEM_LIMIT),
        cost_estimate=pl.CostEstimate(flops=2**20, bytes_accessed=24 * 2**20, transcendentals=0),
        name="split_amplitudes",
    )(*pieces)


def product_kernel(places, has_start, meta_ref, *rest):
    chunk_refs = rest[: len(places)]
    amp_ref = rest[len(places)]
    out_ref = rest[-1]
    me_row = lax.axis_index("row")
    me_col = lax.axis_index("col")
    block = out_ref.shape[0] // 2
    if has_start:
        out_ref[...] = rest[len(places) + 1][...]
    else:
        out_ref[...] = jnp.zeros_like(out_ref)
    for ref, runs in zip(chunk_refs, places):
        at = 0
        for dy, dz, first, count in runs:
            source = ((me_row // Z) ^ dy) * Z + (me_row + dz) % Z

            def step(m, ref=ref, source=source, at=at, first=first):
                number = first + m
                s = number // CHUNK
                code = meta_ref[s * 8, (number % CHUNK) * N_ROW + source]
                column = code // NT_DEV
                away = (column // 4 + 4 - me_col // 4) % 4
                tile = ref[at + m]
                high = tile.astype(jnp.bfloat16)
                low = (tile - high.astype(jnp.float32)).astype(jnp.bfloat16)
                wide = jnp.concatenate([high, low], axis=1)
                wide = jnp.concatenate([wide, wide], axis=0)
                columns = pl.ds(pl.multiple_of((code % NT_DEV) * TILE, TILE), TILE)
                for begin in range(0, out_ref.shape[0], block):
                    rows = pl.ds(begin, block)
                    both = jnp.dot(
                        amp_ref[((column ^ me_col) // 2) % 2, (column ^ me_col) % 2, away, s, rows],
                        wide,
                        preferred_element_type=jnp.float32,
                    )
                    out_ref[rows, columns] += both[:, :TILE] + both[:, TILE:]

            pl.loop(0, count, unroll=min(count, 4))(step)
            at += count


def product(meta, chunks, places, amps, start=None):
    vmem = pl.BlockSpec(memory_space=pltpu.VMEM)
    rows = amps.shape[4]
    operands = list(chunks) + [amps] + ([] if start is None else [start])
    tiles = sum(c.shape[0] for c in chunks)
    return pl.pallas_call(
        functools.partial(product_kernel, places, start is not None),
        out_shape=jax.ShapeDtypeStruct((rows, NT_DEV * TILE), jnp.float32),
        in_specs=[pl.BlockSpec(memory_space=pltpu.SMEM)] + [vmem] * len(operands),
        out_specs=vmem,
        compiler_params=pltpu.CompilerParams(vmem_limit_bytes=VMEM_LIMIT),
        cost_estimate=pl.CostEstimate(
            flops=6 * tiles * rows * 4 * TILE * TILE, bytes_accessed=8 * 2**20, transcendentals=0
        ),
        name="product",
    )(meta, *operands)


def along_z(value, step):
    pairs = [(i, (i // Z) * Z + (i % Z + step) % Z) for i in range(N_ROW)]
    return lax.ppermute(value, "row", pairs)


def across_y(value):
    return lax.ppermute(value, "row", [(i, i ^ Z) for i in range(N_ROW)])


def along_x(value, step):
    pairs = [(c, ((c // 4 + step) % 4) * 4 + c % 4) for c in range(N_COL)]
    return lax.ppermute(value, "col", pairs)


def flip(value, bit):
    return lax.ppermute(value, "col", [(c, c ^ bit) for c in range(N_COL)])


def shards(amplitudes, integrals, tile_rows, tile_reader, tile_column):
    held = (STEPS, tile_rows.shape[1] // LANES, LANES)
    meta, sent = route(
        tile_reader.reshape(held), tile_rows.reshape(held), tile_column.reshape(held), integrals
    )
    side, amp_right, amp_left = flip(amplitudes, 2), along_x(amplitudes, -1), along_x(amplitudes, 1)
    arrived = lax.all_to_all(sent, "col", split_axis=0, concat_axis=0, tiled=True)
    own, side, amp_right, amp_left = compact(meta, arrived, (side, amp_right, amp_left))

    left, right, other = along_z(own, 1), along_z(own, -1), across_y(own)
    side_around = [along_x(side, step) for step in (-1, 2, 1)]
    amp_far = along_x(amp_left, 1)
    flipped = [flip(p, 1) for p in (amplitudes, amp_right, amp_left, side)]

    up, down, across, amp_far, *side_around = regroup(
        [left, right, other],
        [[(0, 0, 8), (2, 0, 8)], [(1, 8, 8), (2, 8, 8)], [(0, 8, 8), (1, 0, 8)]],
        [amp_far] + side_around,
        flipped,
    )
    up, down, across = along_z(up, 1), along_z(down, -1), across_y(across)
    flipped = flipped[:2] + [flip(amp_far, 1)] + flipped[2:] + [flip(p, 1) for p in side_around]
    amps = split_amplitudes([amplitudes, amp_right, amp_far, amp_left] + flipped[:4] + [side] + side_around + flipped[4:])
    places = [[(dy, dz, 0, 16)] for dy, dz in ((0, 0), (0, 3), (0, 1), (1, 0))]
    ladder = product(meta, [own, left, right, other], places, amps)

    far_up, far_down, far_across = regroup(
        [up, down], [[(0, 8, 5)], [(1, 11, 5)], [(0, 5, 3), (1, 0, 3)]], (), [ladder]
    )
    far_up, far_down, far_across = along_z(far_up, 1), along_z(far_down, -1), across_y(far_across)
    places = [
        [(0, 2, 0, 8), (1, 3, 0, 8)],
        [(0, 2, 8, 8), (1, 1, 8, 8)],
        [(1, 3, 8, 8), (1, 1, 0, 8)],
    ]
    ladder = product(meta, [up, down, across], places, amps, ladder)
    places = [[(1, 2, 0, 5)], [(1, 2, 11, 5)], [(1, 2, 5, 6)]]
    return product(meta, [far_up, far_down, far_across], places, amps, ladder)


def solution(mesh):
    return jax.shard_map(
        shards,
        mesh=mesh,
        in_specs=(P(None, "row", "col"), P(None, "col", None, None), P(), P(), P()),
        out_specs=P("row", "col"),
        check_vma=False,
    )
```

```python
import functools

import jax
import jax.numpy as jnp
from jax import lax
from jax.experimental import pallas as pl
from jax.experimental.pallas import tpu as pltpu
from jax.sharding import PartitionSpec as P

TILE = 128
STEPS = 2
NT_DEV = 16
N_COL = 16
N_ROW = 8
Z = 4
HOLD = 64
CHUNK = HOLD // N_ROW
LANES = 128
VMEM_LIMIT = 26 * 1024 * 1024
SMALL_LIMIT = 12 * 1024 * 1024


def route_kernel(reader_ref, row_ref, column_ref, tiles_ref, meta_ref, *rest):
    out_ref, meta_smem, meta_sem, sems = rest
    me_row = lax.axis_index("row")
    me_col = lax.axis_index("col")
    groups = reader_ref.shape[1]
    lane = lax.broadcasted_iota(jnp.int32, (1, LANES), 1)
    upto = (
        lax.broadcasted_iota(jnp.int32, (LANES, LANES), 0)
        <= lax.broadcasted_iota(jnp.int32, (LANES, LANES), 1)
    ).astype(jnp.bfloat16)
    names = lax.broadcasted_iota(jnp.int32, (N_COL, LANES), 0)
    numbers = lax.broadcasted_iota(jnp.int32, (HOLD, LANES), 0)
    ones = jnp.ones((8, LANES), jnp.bfloat16)

    def to_lanes(sums):
        return lax.dot_general(
            ones, sums.astype(jnp.bfloat16), (((1,), (1,)), ((), ())), preferred_element_type=jnp.float32
        )

    for s in range(STEPS):
        readers = reader_ref[s]
        named = [(readers[g : g + 1] == names) for g in range(groups)]
        onehot = jnp.concatenate([n.astype(jnp.bfloat16) for n in named], axis=0)
        within = jnp.dot(onehot, upto, preferred_element_type=jnp.float32)
        before = jnp.zeros((N_COL, 1), jnp.float32)
        send = jnp.zeros((N_COL, LANES), jnp.float32)
        code = jnp.zeros((HOLD, LANES), jnp.float32)
        holder = jnp.zeros((HOLD, LANES), jnp.float32)
        for g in range(groups):
            count = within[g * N_COL : (g + 1) * N_COL]
            number = (count + before - 1.0).astype(jnp.int32)
            before = before + count[:, LANES - 1 :]
            held = lane + g * LANES
            sent = named[g] & (held // HOLD == me_col) & (number % N_ROW == me_row)
            send = send + jnp.where(sent, (held % HOLD).astype(jnp.float32), 0.0)
            place = jnp.sum(jnp.where(named[g], number, 0), axis=0, keepdims=True)
            mine = (place == numbers) & (readers[g : g + 1] == me_col)
            tile_code = row_ref[s, g : g + 1] * NT_DEV + column_ref[s, g : g + 1]
            code = code + jnp.where(mine, tile_code.astype(jnp.float32), 0.0)
            holder = holder + jnp.where(mine, (held // HOLD).astype(jnp.float32), 0.0)
        parts = [to_lanes(code)[:1], to_lanes(holder)[:1], to_lanes(send)[:1]]
        for at, part in enumerate(parts):
            meta_ref[s * 8 + at : s * 8 + at + 1, : part.shape[1]] = part.astype(jnp.int32)
    copy = pltpu.make_async_copy(meta_ref, meta_smem, meta_sem)
    copy.start()
    copy.wait()
    copies = []
    for s in range(STEPS):
        for r in range(N_COL):
            tile = meta_smem[s * 8 + 2, r]
            copies.append(
                pltpu.make_async_copy(tiles_ref.at[s, tile], out_ref.at[r, s], sems.at[len(copies)])
            )
            copies[-1].start()
    for copy in copies:
        copy.wait()


def route(readers, rows, columns, tiles):
    vmem = pl.BlockSpec(memory_space=pltpu.VMEM)
    return pl.pallas_call(
        route_kernel,
        out_shape=(
            jax.ShapeDtypeStruct((8 * STEPS, LANES), jnp.int32),
            jax.ShapeDtypeStruct((N_COL, STEPS, TILE, TILE), jnp.float32),
        ),
        in_specs=[vmem, vmem, vmem, pl.BlockSpec(memory_space=pltpu.HBM)],
        out_specs=(vmem, vmem),
        scratch_shapes=[
            pltpu.SMEM((8 * STEPS, LANES), jnp.int32),
            pltpu.SemaphoreType.DMA,
            pltpu.SemaphoreType.DMA((STEPS * N_COL,)),
        ],
        name="route",
    )(readers, rows, columns, tiles)


def compact_kernel(meta_ref, arrived_ref, amp_ref, side_ref, left_ref, far_ref, out_ref, minus_ref, plus_ref, sems):
    me_row = lax.axis_index("row")
    copies = []

    def copy(source, target):
        copies.append(pltpu.make_async_copy(source, target, sems.at[len(copies)]))
        copies[-1].start()

    for s in range(STEPS):
        for j in range(CHUNK):
            holder = meta_ref[s * 8 + 1, j * N_ROW + me_row]
            copy(arrived_ref.at[holder, s], out_ref.at[s * CHUNK + j])
    for n, ref in enumerate((amp_ref, side_ref)):
        copy(ref, minus_ref.at[pl.ds(n * STEPS, STEPS)])
    for n, ref in enumerate((left_ref, side_ref)):
        copy(ref, plus_ref.at[pl.ds(n * STEPS, STEPS)])
    for one in copies:
        one.wait()


def compact(meta, arrived, amplitudes, side, amp_left, side_far):
    tiles = STEPS * CHUNK
    hbm, vmem = pl.BlockSpec(memory_space=pltpu.HBM), pl.BlockSpec(memory_space=pltpu.VMEM)
    pair = jax.ShapeDtypeStruct((2 * STEPS,) + amplitudes.shape[1:], jnp.float32)
    return pl.pallas_call(
        compact_kernel,
        out_shape=[jax.ShapeDtypeStruct((tiles, TILE, TILE), jnp.float32), pair, pair],
        in_specs=[pl.BlockSpec(memory_space=pltpu.SMEM)] + [hbm] * 5,
        out_specs=[vmem] * 3,
        scratch_shapes=[pltpu.SemaphoreType.DMA((tiles + 4,))],
        compiler_params=pltpu.CompilerParams(vmem_limit_bytes=SMALL_LIMIT),
        name="compact",
    )(meta, arrived, amplitudes, side, amp_left, side_far)


def regroup_kernel(plan, *refs):
    outs, sems = refs[-1 - len(plan) : -1], refs[-1]
    copies = []
    for out, parts in zip(outs, plan):
        begin = 0
        for source, first, size in parts:
            copies.append(
                pltpu.make_async_copy(
                    refs[source].at[pl.ds(first, size)], out.at[pl.ds(begin, size)], sems.at[len(copies)]
                )
            )
            copies[-1].start()
            begin += size
    for copy in copies:
        copy.wait()


def regroup(chunks, plan, *earlier):
    any_space = pl.BlockSpec(memory_space=pl.ANY)
    shapes = [
        (sum(size for _, _, size in parts),) + chunks[parts[0][0]].shape[1:] for parts in plan
    ]
    return pl.pallas_call(
        functools.partial(regroup_kernel, plan),
        out_shape=[jax.ShapeDtypeStruct(shape, jnp.float32) for shape in shapes],
        in_specs=[any_space] * (len(chunks) + len(earlier)),
        out_specs=[pl.BlockSpec(memory_space=pltpu.VMEM)] * len(plan),
        scratch_shapes=[pltpu.SemaphoreType.DMA((sum(len(parts) for parts in plan),))],
        compiler_params=pltpu.CompilerParams(vmem_limit_bytes=SMALL_LIMIT),
        name="regroup",
    )(*chunks, *earlier)


def split_kernel(amp_ref, other_ref, out_ref):
    for core, ref in enumerate((amp_ref, other_ref)):
        for n in range(ref.shape[0]):
            value = ref[n]
            high = value.astype(jnp.bfloat16)
            out_ref[core, n, :, :TILE] = high
            out_ref[core, n, :, TILE:] = (value - high.astype(jnp.float32)).astype(jnp.bfloat16)


def split_amplitudes(ours, others):
    count, rows = ours.shape[:2]
    block = pl.BlockSpec((2, rows, TILE), lambda n: (n, 0, 0))
    return pl.pallas_call(
        split_kernel,
        out_shape=jax.ShapeDtypeStruct((2, count, rows, 2 * TILE), jnp.bfloat16),
        grid=(count // 2,),
        in_specs=[block, block],
        out_specs=pl.BlockSpec((2, 2, rows, 2 * TILE), lambda n: (0, n, 0, 0)),
        compiler_params=pltpu.CompilerParams(vmem_limit_bytes=SMALL_LIMIT),
        cost_estimate=pl.CostEstimate(flops=2**20, bytes_accessed=24 * 2**20, transcendentals=0),
        name="split_amplitudes",
    )(ours, others)


def product_kernel(places, has_start, meta_ref, *rest):
    chunk_refs = rest[: len(places)]
    amp_ref = rest[len(places)]
    out_ref = rest[-1]
    me_row = lax.axis_index("row")
    me_col = lax.axis_index("col")
    block = out_ref.shape[0] // 2
    if has_start:
        out_ref[...] = rest[len(places) + 1][...]
    else:
        out_ref[...] = jnp.zeros_like(out_ref)
    for ref, runs in zip(chunk_refs, places):
        at = 0
        for dy, dz, first, count in runs:
            source = ((me_row // Z) ^ dy) * Z + (me_row + dz) % Z

            def step(m, ref=ref, source=source, at=at, first=first):
                number = first + m
                s = number // CHUNK
                code = meta_ref[s * 8, (number % CHUNK) * N_ROW + source]
                column = code // NT_DEV
                away = ((column // 4 + 4 - me_col // 4) % 4) * 2 + ((column ^ me_col) // 2) % 2
                tile = ref[at + m]
                high = tile.astype(jnp.bfloat16)
                low = (tile - high.astype(jnp.float32)).astype(jnp.bfloat16)
                wide = jnp.concatenate([high, low], axis=1)
                wide = jnp.concatenate([wide, wide], axis=0)
                columns = pl.ds(pl.multiple_of((code % NT_DEV) * TILE, TILE), TILE)
                for begin in range(0, out_ref.shape[0], block):
                    rows = pl.ds(begin, block)
                    both = jnp.dot(
                        amp_ref[(column ^ me_col) % 2, away * STEPS + s, rows],
                        wide,
                        preferred_element_type=jnp.float32,
                    )
                    out_ref[rows, columns] += both[:, :TILE] + both[:, TILE:]

            pl.loop(0, count, unroll=min(count, 4))(step)
            at += count


def product(meta, chunks, places, amps, start=None):
    vmem = pl.BlockSpec(memory_space=pltpu.VMEM)
    rows = amps.shape[2]
    operands = list(chunks) + [amps] + ([] if start is None else [start])
    tiles = sum(c.shape[0] for c in chunks)
    return pl.pallas_call(
        functools.partial(product_kernel, places, start is not None),
        out_shape=jax.ShapeDtypeStruct((rows, NT_DEV * TILE), jnp.float32),
        in_specs=[pl.BlockSpec(memory_space=pltpu.SMEM)] + [vmem] * len(operands),
        out_specs=vmem,
        compiler_params=pltpu.CompilerParams(vmem_limit_bytes=VMEM_LIMIT),
        cost_estimate=pl.CostEstimate(
            flops=6 * tiles * rows * 4 * TILE * TILE, bytes_accessed=8 * 2**20, transcendentals=0
        ),
        name="product",
    )(meta, *operands)


def along_z(value, step):
    pairs = [(i, (i // Z) * Z + (i % Z + step) % Z) for i in range(N_ROW)]
    return lax.ppermute(value, "row", pairs)


def across_y(value):
    return lax.ppermute(value, "row", [(i, i ^ Z) for i in range(N_ROW)])


def along_x(value, step):
    pairs = [(c, ((c // 4 + step) % 4) * 4 + c % 4) for c in range(N_COL)]
    return lax.ppermute(value, "col", pairs)


def flip(value, bit):
    return lax.ppermute(value, "col", [(c, c ^ bit) for c in range(N_COL)])


def shards(amplitudes, integrals, tile_rows, tile_reader, tile_column):
    held = (STEPS, tile_rows.shape[1] // LANES, LANES)
    meta, sent = route(
        tile_reader.reshape(held), tile_rows.reshape(held), tile_column.reshape(held), integrals
    )
    side, amp_left = flip(amplitudes, 2), along_x(amplitudes, 1)
    side_far = lax.ppermute(amplitudes, "col", [(c, (c ^ 2) ^ 8) for c in range(N_COL)])
    arrived = lax.all_to_all(sent, "col", split_axis=0, concat_axis=0, tiled=True)
    own, minus, plus = compact(meta, arrived, amplitudes, side, amp_left, side_far)

    left, right, other = along_z(own, 1), along_z(own, -1), across_y(own)
    from_right, from_left = along_x(minus, -1), along_x(plus, 1)

    up, down, across, ours = regroup(
        [left, right, other, minus, from_right, from_left, side_far, plus],
        [
            [(0, 0, 8), (2, 0, 8)],
            [(1, 8, 8), (2, 8, 8)],
            [(0, 8, 8), (1, 0, 8)],
            [(3, 0, 4), (4, 0, 4), (5, 0, 2), (6, 0, 2), (7, 0, 2), (5, 2, 2)],
        ],
    )
    up, down, across = along_z(up, 1), along_z(down, -1), across_y(across)
    amps = split_amplitudes(ours, flip(ours, 1))
    places = [[(dy, dz, 0, 16)] for dy, dz in ((0, 0), (0, 3), (0, 1), (1, 0))]
    ladder = product(meta, [own, left, right, other], places, amps)

    far_up, far_down, far_across = regroup(
        [up, down], [[(0, 8, 5)], [(1, 11, 5)], [(0, 5, 3), (1, 0, 3)]], ladder
    )
    far_up, far_down, far_across = along_z(far_up, 1), along_z(far_down, -1), across_y(far_across)
    places = [
        [(0, 2, 0, 8), (1, 3, 0, 8)],
        [(0, 2, 8, 8), (1, 1, 8, 8)],
        [(1, 3, 8, 8), (1, 1, 0, 8)],
    ]
    ladder = product(meta, [up, down, across], places, amps, ladder)
    places = [[(1, 2, 0, 5)], [(1, 2, 11, 5)], [(1, 2, 5, 6)]]
    return product(meta, [far_up, far_down, far_across], places, amps, ladder)


def solution(mesh):
    return jax.shard_map(
        shards,
        mesh=mesh,
        in_specs=(P(None, "row", "col"), P(None, "col", None, None), P(), P(), P()),
        out_specs=P("row", "col"),
        check_vma=False,
    )
```

```python
import functools

import jax
import jax.numpy as jnp
from jax import lax
from jax.experimental import pallas as pl
from jax.experimental.pallas import tpu as pltpu
from jax.sharding import PartitionSpec as P

TILE = 128
STEPS = 2
NT_DEV = 16
N_COL = 16
N_ROW = 8
Z = 4
HOLD = 64
CHUNK = HOLD // N_ROW
LANES = 128
VMEM_LIMIT = 26 * 1024 * 1024
SMALL_LIMIT = 12 * 1024 * 1024


def route_kernel(reader_ref, row_ref, column_ref, tiles_ref, meta_ref, *rest):
    out_ref, meta_smem, meta_sem, sems = rest
    me_row = lax.axis_index("row")
    me_col = lax.axis_index("col")
    groups = reader_ref.shape[1]
    lane = lax.broadcasted_iota(jnp.int32, (1, LANES), 1)
    upto = (
        lax.broadcasted_iota(jnp.int32, (LANES, LANES), 0)
        <= lax.broadcasted_iota(jnp.int32, (LANES, LANES), 1)
    ).astype(jnp.bfloat16)
    names = lax.broadcasted_iota(jnp.int32, (N_COL, LANES), 0)
    numbers = lax.broadcasted_iota(jnp.int32, (HOLD, LANES), 0)
    ones = jnp.ones((8, LANES), jnp.bfloat16)

    def to_lanes(sums):
        return lax.dot_general(
            ones, sums.astype(jnp.bfloat16), (((1,), (1,)), ((), ())), preferred_element_type=jnp.float32
        )

    for s in range(STEPS):
        readers = reader_ref[s]
        named = [(readers[g : g + 1] == names) for g in range(groups)]
        onehot = jnp.concatenate([n.astype(jnp.bfloat16) for n in named], axis=0)
        within = jnp.dot(onehot, upto, preferred_element_type=jnp.float32)
        before = jnp.zeros((N_COL, 1), jnp.float32)
        send = jnp.zeros((N_COL, LANES), jnp.float32)
        code = jnp.zeros((HOLD, LANES), jnp.float32)
        holder = jnp.zeros((HOLD, LANES), jnp.float32)
        for g in range(groups):
            count = within[g * N_COL : (g + 1) * N_COL]
            number = (count + before - 1.0).astype(jnp.int32)
            before = before + count[:, LANES - 1 :]
            held = lane + g * LANES
            sent = named[g] & (held // HOLD == me_col) & (number % N_ROW == me_row)
            send = send + jnp.where(sent, (held % HOLD).astype(jnp.float32), 0.0)
            place = jnp.sum(jnp.where(named[g], number, 0), axis=0, keepdims=True)
            mine = (place == numbers) & (readers[g : g + 1] == me_col)
            tile_code = row_ref[s, g : g + 1] * NT_DEV + column_ref[s, g : g + 1]
            code = code + jnp.where(mine, tile_code.astype(jnp.float32), 0.0)
            holder = holder + jnp.where(mine, (held // HOLD).astype(jnp.float32), 0.0)
        parts = [to_lanes(code)[:1], to_lanes(holder)[:1], to_lanes(send)[:1]]
        for at, part in enumerate(parts):
            meta_ref[s * 8 + at : s * 8 + at + 1, : part.shape[1]] = part.astype(jnp.int32)
    copy = pltpu.make_async_copy(meta_ref, meta_smem, meta_sem)
    copy.start()
    copy.wait()
    copies = []
    for s in range(STEPS):
        for r in range(N_COL):
            tile = meta_smem[s * 8 + 2, r]
            copies.append(
                pltpu.make_async_copy(tiles_ref.at[s, tile], out_ref.at[r, s], sems.at[len(copies)])
            )
            copies[-1].start()
    for copy in copies:
        copy.wait()


def route(readers, rows, columns, tiles):
    vmem = pl.BlockSpec(memory_space=pltpu.VMEM)
    return pl.pallas_call(
        route_kernel,
        out_shape=(
            jax.ShapeDtypeStruct((8 * STEPS, LANES), jnp.int32),
            jax.ShapeDtypeStruct((N_COL, STEPS, TILE, TILE), jnp.float32),
        ),
        in_specs=[vmem, vmem, vmem, pl.BlockSpec(memory_space=pltpu.HBM)],
        out_specs=(vmem, vmem),
        scratch_shapes=[
            pltpu.SMEM((8 * STEPS, LANES), jnp.int32),
            pltpu.SemaphoreType.DMA,
            pltpu.SemaphoreType.DMA((STEPS * N_COL,)),
        ],
        name="route",
    )(readers, rows, columns, tiles)


def compact_kernel(meta_ref, arrived_ref, amp_ref, side_ref, left_ref, out_ref, minus_ref, plus_ref, sems):
    me_row = lax.axis_index("row")
    copies = []

    def copy(source, target):
        copies.append(pltpu.make_async_copy(source, target, sems.at[len(copies)]))
        copies[-1].start()

    for s in range(STEPS):
        for j in range(CHUNK):
            holder = meta_ref[s * 8 + 1, j * N_ROW + me_row]
            copy(arrived_ref.at[holder, s], out_ref.at[s * CHUNK + j])
    for n, ref in enumerate((amp_ref, side_ref)):
        copy(ref, minus_ref.at[pl.ds(n * STEPS, STEPS)])
    for n, ref in enumerate((left_ref, side_ref)):
        copy(ref, plus_ref.at[pl.ds(n * STEPS, STEPS)])
    for one in copies:
        one.wait()


def compact(meta, arrived, amplitudes, side, amp_left):
    tiles = STEPS * CHUNK
    hbm, vmem = pl.BlockSpec(memory_space=pltpu.HBM), pl.BlockSpec(memory_space=pltpu.VMEM)
    pair = jax.ShapeDtypeStruct((2 * STEPS,) + amplitudes.shape[1:], jnp.float32)
    return pl.pallas_call(
        compact_kernel,
        out_shape=[jax.ShapeDtypeStruct((tiles, TILE, TILE), jnp.float32), pair, pair],
        in_specs=[pl.BlockSpec(memory_space=pltpu.SMEM)] + [hbm] * 4,
        out_specs=[vmem] * 3,
        scratch_shapes=[pltpu.SemaphoreType.DMA((tiles + 4,))],
        compiler_params=pltpu.CompilerParams(vmem_limit_bytes=SMALL_LIMIT),
        name="compact",
    )(meta, arrived, amplitudes, side, amp_left)


def regroup_kernel(plan, *refs):
    outs, sems = refs[-1 - len(plan) : -1], refs[-1]
    copies = []
    for out, parts in zip(outs, plan):
        begin = 0
        for source, first, size in parts:
            copies.append(
                pltpu.make_async_copy(
                    refs[source].at[pl.ds(first, size)], out.at[pl.ds(begin, size)], sems.at[len(copies)]
                )
            )
            copies[-1].start()
            begin += size
    for copy in copies:
        copy.wait()


def regroup(chunks, plan, *earlier):
    any_space = pl.BlockSpec(memory_space=pl.ANY)
    shapes = [
        (sum(size for _, _, size in parts),) + chunks[parts[0][0]].shape[1:] for parts in plan
    ]
    return pl.pallas_call(
        functools.partial(regroup_kernel, plan),
        out_shape=[jax.ShapeDtypeStruct(shape, jnp.float32) for shape in shapes],
        in_specs=[any_space] * (len(chunks) + len(earlier)),
        out_specs=[pl.BlockSpec(memory_space=pltpu.VMEM)] * len(plan),
        scratch_shapes=[pltpu.SemaphoreType.DMA((sum(len(parts) for parts in plan),))],
        compiler_params=pltpu.CompilerParams(vmem_limit_bytes=SMALL_LIMIT),
        name="regroup",
    )(*chunks, *earlier)


def split_kernel(*refs):
    out_ref = refs[-1]
    count = len(refs) // 2
    for core in range(2):
        at = 0
        for ref in refs[core * count : (core + 1) * count]:
            for n in range(ref.shape[0]):
                value = ref[n]
                high = value.astype(jnp.bfloat16)
                out_ref[core, at, :, :TILE] = high
                out_ref[core, at, :, TILE:] = (value - high.astype(jnp.float32)).astype(jnp.bfloat16)
                at += 1


def split_amplitudes(ours, others):
    count, rows = sum(p.shape[0] for p in ours), ours[0].shape[1]
    blocks = [pl.BlockSpec((p.shape[0], rows // 8, TILE), lambda n: (0, n, 0)) for p in ours]
    return pl.pallas_call(
        split_kernel,
        out_shape=jax.ShapeDtypeStruct((2, count, rows, 2 * TILE), jnp.bfloat16),
        grid=(8,),
        in_specs=blocks * 2,
        out_specs=pl.BlockSpec((2, count, rows // 8, 2 * TILE), lambda n: (0, 0, n, 0)),
        compiler_params=pltpu.CompilerParams(vmem_limit_bytes=SMALL_LIMIT),
        cost_estimate=pl.CostEstimate(flops=2**20, bytes_accessed=2**20, transcendentals=0),
        name="split_amplitudes",
    )(*ours, *others)


def product_kernel(places, has_start, meta_ref, *rest):
    chunk_refs = rest[: len(places)]
    amp_ref = rest[len(places)]
    out_ref = rest[-1]
    me_row = lax.axis_index("row")
    me_col = lax.axis_index("col")
    block = out_ref.shape[0] // 2
    if has_start:
        out_ref[...] = rest[len(places) + 1][...]
    else:
        out_ref[...] = jnp.zeros_like(out_ref)
    for ref, runs in zip(chunk_refs, places):
        at = 0
        for dy, dz, first, count in runs:
            source = ((me_row // Z) ^ dy) * Z + (me_row + dz) % Z

            def step(m, ref=ref, source=source, at=at, first=first):
                number = first + m
                s = number // CHUNK
                code = meta_ref[s * 8, (number % CHUNK) * N_ROW + source]
                column = code // NT_DEV
                steps = (column // 4 + 4 - me_col // 4) % 4
                away = (steps ^ (steps // 2)) * 2 + ((column ^ me_col) // 2) % 2
                tile = ref[at + m]
                high = tile.astype(jnp.bfloat16)
                low = (tile - high.astype(jnp.float32)).astype(jnp.bfloat16)
                wide = jnp.concatenate([high, low], axis=1)
                wide = jnp.concatenate([wide, wide], axis=0)
                columns = pl.ds(pl.multiple_of((code % NT_DEV) * TILE, TILE), TILE)
                for begin in range(0, out_ref.shape[0], block):
                    rows = pl.ds(begin, block)
                    both = jnp.dot(
                        amp_ref[(column ^ me_col) % 2, away * STEPS + s, rows],
                        wide,
                        preferred_element_type=jnp.float32,
                    )
                    out_ref[rows, columns] += both[:, :TILE] + both[:, TILE:]

            pl.loop(0, count, unroll=min(count, 4))(step)
            at += count


def product(meta, chunks, places, amps, start=None):
    vmem = pl.BlockSpec(memory_space=pltpu.VMEM)
    rows = amps.shape[2]
    operands = list(chunks) + [amps] + ([] if start is None else [start])
    tiles = sum(c.shape[0] for c in chunks)
    return pl.pallas_call(
        functools.partial(product_kernel, places, start is not None),
        out_shape=jax.ShapeDtypeStruct((rows, NT_DEV * TILE), jnp.float32),
        in_specs=[pl.BlockSpec(memory_space=pltpu.SMEM)] + [vmem] * len(operands),
        out_specs=vmem,
        compiler_params=pltpu.CompilerParams(vmem_limit_bytes=VMEM_LIMIT),
        cost_estimate=pl.CostEstimate(
            flops=tiles * rows * TILE, bytes_accessed=2**20, transcendentals=0
        ),
        name="product",
    )(meta, *operands)


def along_z(value, step):
    pairs = [(i, (i // Z) * Z + (i % Z + step) % Z) for i in range(N_ROW)]
    return lax.ppermute(value, "row", pairs)


def across_y(value):
    return lax.ppermute(value, "row", [(i, i ^ Z) for i in range(N_ROW)])


def along_x(value, step):
    pairs = [(c, ((c // 4 + step) % 4) * 4 + c % 4) for c in range(N_COL)]
    return lax.ppermute(value, "col", pairs)


def flip(value, bit):
    return lax.ppermute(value, "col", [(c, c ^ bit) for c in range(N_COL)])


def shards(amplitudes, integrals, tile_rows, tile_reader, tile_column):
    held = (STEPS, tile_rows.shape[1] // LANES, LANES)
    meta, sent = route(
        tile_reader.reshape(held), tile_rows.reshape(held), tile_column.reshape(held), integrals
    )
    side, amp_left = flip(amplitudes, 2), along_x(amplitudes, 1)
    arrived = lax.all_to_all(sent, "col", split_axis=0, concat_axis=0, tiled=True)
    own, minus, plus = compact(meta, arrived, amplitudes, side, amp_left)

    left, right, other = along_z(own, 1), along_z(own, -1), across_y(own)
    from_right, from_left = along_x(minus, -1), along_x(plus, 1)

    up, down, across, side_far, ours = regroup(
        [left, right, other, minus, from_right, from_left, plus],
        [
            [(0, 0, 8), (2, 0, 8)],
            [(1, 8, 8), (2, 8, 8)],
            [(0, 8, 8), (1, 0, 8)],
            [(4, 2, 2)],
            [(3, 0, 4), (4, 0, 4), (6, 0, 2), (5, 2, 2), (5, 0, 2)],
        ],
    )
    up, down, across = along_z(up, 1), along_z(down, -1), across_y(across)
    ours = [ours, along_x(side_far, -1)]
    amps = split_amplitudes(ours, [flip(p, 1) for p in ours])
    places = [[(dy, dz, 0, 16)] for dy, dz in ((0, 0), (0, 3), (0, 1), (1, 0))]
    ladder = product(meta, [own, left, right, other], places, amps)

    far_up, far_down, far_across = regroup([up, down], [[(0, 8, 5)], [(1, 11, 5)], [(0, 5, 3), (1, 0, 3)]], ladder)
    far_up, far_down, far_across = along_z(far_up, 1), along_z(far_down, -1), across_y(far_across)
    places = [
        [(0, 2, 0, 8), (1, 3, 0, 8)],
        [(0, 2, 8, 8), (1, 1, 8, 8)],
        [(1, 3, 8, 8), (1, 1, 0, 8)],
    ]
    ladder = product(meta, [up, down, across], places, amps, ladder)
    places = [[(1, 2, 0, 5)], [(1, 2, 11, 5)], [(1, 2, 5, 6)]]
    return product(meta, [far_up, far_down, far_across], places, amps, ladder)


def solution(mesh):
    return jax.shard_map(
        shards,
        mesh=mesh,
        in_specs=(P(None, "row", "col"), P(None, "col", None, None), P(), P(), P()),
        out_specs=P("row", "col"),
        check_vma=False,
    )
```

```python
import functools

import jax
import jax.numpy as jnp
from jax import lax
from jax.experimental import pallas as pl
from jax.experimental.pallas import tpu as pltpu
from jax.sharding import PartitionSpec as P

TILE = 128
STEPS = 2
NT_DEV = 16
N_COL = 16
N_ROW = 8
Z = 4
HOLD = 64
CHUNK = HOLD // N_ROW
LANES = 128
VMEM_LIMIT = 26 * 1024 * 1024
SMALL_LIMIT = 12 * 1024 * 1024


def route_kernel(reader_ref, row_ref, column_ref, tiles_ref, meta_ref, *rest):
    out_ref, meta_smem, meta_sem, sems = rest
    me_row = lax.axis_index("row")
    me_col = lax.axis_index("col")
    groups = reader_ref.shape[1]
    lane = lax.broadcasted_iota(jnp.int32, (1, LANES), 1)
    upto = (
        lax.broadcasted_iota(jnp.int32, (LANES, LANES), 0)
        <= lax.broadcasted_iota(jnp.int32, (LANES, LANES), 1)
    ).astype(jnp.bfloat16)
    names = lax.broadcasted_iota(jnp.int32, (N_COL, LANES), 0)
    numbers = lax.broadcasted_iota(jnp.int32, (HOLD, LANES), 0)
    ones = jnp.ones((8, LANES), jnp.bfloat16)

    def to_lanes(sums):
        return lax.dot_general(
            ones, sums.astype(jnp.bfloat16), (((1,), (1,)), ((), ())), preferred_element_type=jnp.float32
        )

    for s in range(STEPS):
        readers = reader_ref[s]
        named = [(readers[g : g + 1] == names) for g in range(groups)]
        onehot = jnp.concatenate([n.astype(jnp.bfloat16) for n in named], axis=0)
        within = jnp.dot(onehot, upto, preferred_element_type=jnp.float32)
        before = jnp.zeros((N_COL, 1), jnp.float32)
        send = jnp.zeros((N_COL, LANES), jnp.float32)
        code = jnp.zeros((HOLD, LANES), jnp.float32)
        holder = jnp.zeros((HOLD, LANES), jnp.float32)
        for g in range(groups):
            count = within[g * N_COL : (g + 1) * N_COL]
            number = (count + before - 1.0).astype(jnp.int32)
            before = before + count[:, LANES - 1 :]
            held = lane + g * LANES
            sent = named[g] & (held // HOLD == me_col) & (number % N_ROW == me_row)
            send = send + jnp.where(sent, (held % HOLD).astype(jnp.float32), 0.0)
            place = jnp.sum(jnp.where(named[g], number, 0), axis=0, keepdims=True)
            mine = (place == numbers) & (readers[g : g + 1] == me_col)
            tile_code = row_ref[s, g : g + 1] * NT_DEV + column_ref[s, g : g + 1]
            code = code + jnp.where(mine, tile_code.astype(jnp.float32), 0.0)
            holder = holder + jnp.where(mine, (held // HOLD).astype(jnp.float32), 0.0)
        parts = [to_lanes(code)[:1], to_lanes(holder)[:1], to_lanes(send)[:1]]
        for at, part in enumerate(parts):
            meta_ref[s * 8 + at : s * 8 + at + 1, : part.shape[1]] = part.astype(jnp.int32)
    copy = pltpu.make_async_copy(meta_ref, meta_smem, meta_sem)
    copy.start()
    copy.wait()
    copies = []
    for s in range(STEPS):
        for r in range(N_COL):
            tile = meta_smem[s * 8 + 2, r]
            copies.append(
                pltpu.make_async_copy(tiles_ref.at[s, tile], out_ref.at[r, s], sems.at[len(copies)])
            )
            copies[-1].start()
    for copy in copies:
        copy.wait()


def route(readers, rows, columns, tiles):
    vmem = pl.BlockSpec(memory_space=pltpu.VMEM)
    return pl.pallas_call(
        route_kernel,
        out_shape=(
            jax.ShapeDtypeStruct((8 * STEPS, LANES), jnp.int32),
            jax.ShapeDtypeStruct((N_COL, STEPS, TILE, TILE), jnp.float32),
        ),
        in_specs=[vmem, vmem, vmem, pl.BlockSpec(memory_space=pltpu.HBM)],
        out_specs=(vmem, vmem),
        scratch_shapes=[
            pltpu.SMEM((8 * STEPS, LANES), jnp.int32),
            pltpu.SemaphoreType.DMA,
            pltpu.SemaphoreType.DMA((STEPS * N_COL,)),
        ],
        name="route",
    )(readers, rows, columns, tiles)


def compact_kernel(meta_ref, arrived_ref, amp_ref, side_ref, left_ref, out_ref, minus_ref, plus_ref, sems):
    me_row = lax.axis_index("row")
    copies = []

    def copy(source, target):
        copies.append(pltpu.make_async_copy(source, target, sems.at[len(copies)]))
        copies[-1].start()

    for s in range(STEPS):
        for j in range(CHUNK):
            holder = meta_ref[s * 8 + 1, j * N_ROW + me_row]
            copy(arrived_ref.at[holder, s], out_ref.at[s * CHUNK + j])
    for n, ref in enumerate((amp_ref, side_ref)):
        copy(ref, minus_ref.at[pl.ds(n * STEPS, STEPS)])
    for n, ref in enumerate((left_ref, side_ref)):
        copy(ref, plus_ref.at[pl.ds(n * STEPS, STEPS)])
    for one in copies:
        one.wait()


def compact(meta, arrived, amplitudes, side, amp_left):
    tiles = STEPS * CHUNK
    hbm, vmem = pl.BlockSpec(memory_space=pltpu.HBM), pl.BlockSpec(memory_space=pltpu.VMEM)
    pair = jax.ShapeDtypeStruct((2 * STEPS,) + amplitudes.shape[1:], jnp.float32)
    return pl.pallas_call(
        compact_kernel,
        out_shape=[jax.ShapeDtypeStruct((tiles, TILE, TILE), jnp.float32), pair, pair],
        in_specs=[pl.BlockSpec(memory_space=pltpu.SMEM)] + [hbm] * 4,
        out_specs=[vmem] * 3,
        scratch_shapes=[pltpu.SemaphoreType.DMA((tiles + 4,))],
        compiler_params=pltpu.CompilerParams(vmem_limit_bytes=SMALL_LIMIT),
        name="compact",
    )(meta, arrived, amplitudes, side, amp_left)


def regroup_kernel(plan, *refs):
    outs, sems = refs[-1 - len(plan) : -1], refs[-1]
    copies = []
    for out, parts in zip(outs, plan):
        begin = 0
        for source, first, size in parts:
            copies.append(
                pltpu.make_async_copy(
                    refs[source].at[pl.ds(first, size)], out.at[pl.ds(begin, size)], sems.at[len(copies)]
                )
            )
            copies[-1].start()
            begin += size
    for copy in copies:
        copy.wait()


def regroup(chunks, plan, *earlier):
    any_space = pl.BlockSpec(memory_space=pl.ANY)
    shapes = [
        (sum(size for _, _, size in parts),) + chunks[parts[0][0]].shape[1:] for parts in plan
    ]
    return pl.pallas_call(
        functools.partial(regroup_kernel, plan),
        out_shape=[jax.ShapeDtypeStruct(shape, jnp.float32) for shape in shapes],
        in_specs=[any_space] * (len(chunks) + len(earlier)),
        out_specs=[pl.BlockSpec(memory_space=pltpu.VMEM)] * len(plan),
        scratch_shapes=[pltpu.SemaphoreType.DMA((sum(len(parts) for parts in plan),))],
        compiler_params=pltpu.CompilerParams(vmem_limit_bytes=SMALL_LIMIT),
        name="regroup",
    )(*chunks, *earlier)


def split_kernel(*refs):
    out_ref = refs[-1]
    count = len(refs) // 2
    for core in range(2):
        at = 0
        for ref in refs[core * count : (core + 1) * count]:
            for n in range(ref.shape[0]):
                value = ref[n]
                high = value.astype(jnp.bfloat16)
                out_ref[core, at, :, :TILE] = high
                out_ref[core, at, :, TILE:] = (value - high.astype(jnp.float32)).astype(jnp.bfloat16)
                at += 1


def split_amplitudes(ours, others):
    count, rows = sum(p.shape[0] for p in ours), ours[0].shape[1]
    blocks = [pl.BlockSpec((p.shape[0], rows // 8, TILE), lambda n: (0, n, 0)) for p in ours]
    return pl.pallas_call(
        split_kernel,
        out_shape=jax.ShapeDtypeStruct((2, count, rows, 2 * TILE), jnp.bfloat16),
        grid=(8,),
        in_specs=blocks * 2,
        out_specs=pl.BlockSpec((2, count, rows // 8, 2 * TILE), lambda n: (0, 0, n, 0)),
        compiler_params=pltpu.CompilerParams(vmem_limit_bytes=SMALL_LIMIT),
        cost_estimate=pl.CostEstimate(flops=2**20, bytes_accessed=2**20, transcendentals=0),
        name="split_amplitudes",
    )(*ours, *others)


def product_kernel(places, has_start, meta_ref, *rest):
    chunk_refs = rest[: len(places)]
    amp_ref = rest[len(places)]
    out_ref = rest[-1]
    me_row = lax.axis_index("row")
    me_col = lax.axis_index("col")
    block = out_ref.shape[0] // 2
    if has_start:
        out_ref[...] = rest[len(places) + 1][...]
    else:
        out_ref[...] = jnp.zeros_like(out_ref)
    for ref, runs in zip(chunk_refs, places):
        at = 0
        for dy, dz, first, count in runs:
            source = ((me_row // Z) ^ dy) * Z + (me_row + dz) % Z

            def step(m, ref=ref, source=source, at=at, first=first):
                number = first + m
                s = number // CHUNK
                code = meta_ref[s * 8, (number % CHUNK) * N_ROW + source]
                column = code // NT_DEV
                steps = (column // 4 + 4 - me_col // 4) % 4
                away = (steps ^ (steps // 2)) * 2 + ((column ^ me_col) // 2) % 2
                tile = ref[at + m]
                high = tile.astype(jnp.bfloat16)
                low = (tile - high.astype(jnp.float32)).astype(jnp.bfloat16)
                wide = jnp.concatenate([high, low], axis=1)
                wide = jnp.concatenate([wide, wide], axis=0)
                columns = pl.ds(pl.multiple_of((code % NT_DEV) * TILE, TILE), TILE)
                for begin in range(0, out_ref.shape[0], block):
                    rows = pl.ds(begin, block)
                    both = jnp.dot(
                        amp_ref[(column ^ me_col) % 2, away * STEPS + s, rows],
                        wide,
                        preferred_element_type=jnp.float32,
                    )
                    out_ref[rows, columns] += both[:, :TILE] + both[:, TILE:]

            pl.loop(0, count, unroll=4 if count % 4 == 0 else count)(step)
            at += count


def product(meta, chunks, places, amps, start=None):
    vmem = pl.BlockSpec(memory_space=pltpu.VMEM)
    rows = amps.shape[2]
    operands = list(chunks) + [amps] + ([] if start is None else [start])
    tiles = sum(c.shape[0] for c in chunks)
    return pl.pallas_call(
        functools.partial(product_kernel, places, start is not None),
        out_shape=jax.ShapeDtypeStruct((rows, NT_DEV * TILE), jnp.float32),
        in_specs=[pl.BlockSpec(memory_space=pltpu.SMEM)] + [vmem] * len(operands),
        out_specs=vmem,
        compiler_params=pltpu.CompilerParams(vmem_limit_bytes=VMEM_LIMIT),
        cost_estimate=pl.CostEstimate(
            flops=tiles * rows * TILE, bytes_accessed=2**20, transcendentals=0
        ),
        name="product",
    )(meta, *operands)


def along_z(value, step):
    pairs = [(i, (i // Z) * Z + (i % Z + step) % Z) for i in range(N_ROW)]
    return lax.ppermute(value, "row", pairs)


def across_y(value):
    return lax.ppermute(value, "row", [(i, i ^ Z) for i in range(N_ROW)])


def along_x(value, step):
    pairs = [(c, ((c // 4 + step) % 4) * 4 + c % 4) for c in range(N_COL)]
    return lax.ppermute(value, "col", pairs)


def flip(value, bit):
    return lax.ppermute(value, "col", [(c, c ^ bit) for c in range(N_COL)])


def shards(amplitudes, integrals, tile_rows, tile_reader, tile_column):
    held = (STEPS, tile_rows.shape[1] // LANES, LANES)
    meta, sent = route(
        tile_reader.reshape(held), tile_rows.reshape(held), tile_column.reshape(held), integrals
    )
    side, amp_left = flip(amplitudes, 2), along_x(amplitudes, 1)
    arrived = lax.all_to_all(sent, "col", split_axis=0, concat_axis=0, tiled=True)
    own, minus, plus = compact(meta, arrived, amplitudes, side, amp_left)

    left, right, other = along_z(own, 1), along_z(own, -1), across_y(own)
    from_right, from_left = along_x(minus, -1), along_x(plus, 1)

    up, down, across, side_far, ours = regroup(
        [left, right, other, minus, from_right, from_left, plus],
        [
            [(0, 0, 8), (2, 0, 8)],
            [(1, 8, 8), (2, 8, 8)],
            [(0, 8, 8), (1, 0, 8)],
            [(4, 2, 2)],
            [(3, 0, 4), (4, 0, 4), (6, 0, 2), (5, 2, 2), (5, 0, 2)],
        ],
    )
    up, down, across = along_z(up, 1), along_z(down, -1), across_y(across)
    ours = [ours, along_x(side_far, -1)]
    amps = split_amplitudes(ours, [flip(p, 1) for p in ours])
    places = [[(dy, dz, 0, 16)] for dy, dz in ((0, 0), (0, 3), (0, 1), (1, 0))]
    ladder = product(meta, [own, left, right, other], places, amps)

    far_up, far_down, far_across = regroup([up, down], [[(0, 8, 5)], [(1, 11, 5)], [(0, 5, 3), (1, 0, 3)]], ladder)
    far_up, far_down, far_across = along_z(far_up, 1), along_z(far_down, -1), across_y(far_across)
    places = [
        [(0, 2, 0, 8), (1, 3, 0, 8)],
        [(0, 2, 8, 8), (1, 1, 8, 8)],
        [(1, 3, 8, 8), (1, 1, 0, 8)],
    ]
    ladder = product(meta, [up, down, across], places, amps, ladder)
    places = [[(1, 2, 0, 5)], [(1, 2, 11, 5)], [(1, 2, 5, 6)]]
    return product(meta, [far_up, far_down, far_across], places, amps, ladder)


def solution(mesh):
    return jax.shard_map(
        shards,
        mesh=mesh,
        in_specs=(P(None, "row", "col"), P(None, "col", None, None), P(), P(), P()),
        out_specs=P("row", "col"),
        check_vma=False,
    )
```

```python
import functools

import jax
import jax.numpy as jnp
from jax import lax
from jax.experimental import pallas as pl
from jax.experimental.pallas import tpu as pltpu
from jax.sharding import PartitionSpec as P

TILE = 128
STEPS = 2
NT_DEV = 16
N_COL = 16
N_ROW = 8
Z = 4
HOLD = 64
CHUNK = HOLD // N_ROW
LANES = 128
VMEM_LIMIT = 26 * 1024 * 1024
SMALL_LIMIT = 12 * 1024 * 1024


def route_kernel(reader_ref, row_ref, column_ref, tiles_ref, meta_ref, *rest):
    out_ref, meta_smem, meta_sem, sems = rest
    me_row = lax.axis_index("row")
    me_col = lax.axis_index("col")
    groups = reader_ref.shape[1]
    lane = lax.broadcasted_iota(jnp.int32, (1, LANES), 1)
    upto = (
        lax.broadcasted_iota(jnp.int32, (LANES, LANES), 0)
        <= lax.broadcasted_iota(jnp.int32, (LANES, LANES), 1)
    ).astype(jnp.bfloat16)
    names = lax.broadcasted_iota(jnp.int32, (N_COL, LANES), 0)
    numbers = lax.broadcasted_iota(jnp.int32, (HOLD, LANES), 0)
    ones = jnp.ones((8, LANES), jnp.bfloat16)

    def to_lanes(sums):
        return lax.dot_general(
            ones, sums.astype(jnp.bfloat16), (((1,), (1,)), ((), ())), preferred_element_type=jnp.float32
        )

    for s in range(STEPS):
        readers = reader_ref[s]
        named = [(readers[g : g + 1] == names) for g in range(groups)]
        onehot = jnp.concatenate([n.astype(jnp.bfloat16) for n in named], axis=0)
        within = jnp.dot(onehot, upto, preferred_element_type=jnp.float32)
        before = jnp.zeros((N_COL, 1), jnp.float32)
        send = jnp.zeros((N_COL, LANES), jnp.float32)
        code = jnp.zeros((HOLD, LANES), jnp.float32)
        holder = jnp.zeros((HOLD, LANES), jnp.float32)
        for g in range(groups):
            count = within[g * N_COL : (g + 1) * N_COL]
            number = (count + before - 1.0).astype(jnp.int32)
            before = before + count[:, LANES - 1 :]
            held = lane + g * LANES
            sent = named[g] & (held // HOLD == me_col) & (number % N_ROW == me_row)
            send = send + jnp.where(sent, (held % HOLD).astype(jnp.float32), 0.0)
            place = jnp.sum(jnp.where(named[g], number, 0), axis=0, keepdims=True)
            mine = (place == numbers) & (readers[g : g + 1] == me_col)
            panel, lanes = slice(s, s + 1), slice(g * LANES, (g + 1) * LANES)
            tile_code = row_ref[panel, lanes] * NT_DEV + column_ref[panel, lanes]
            code = code + jnp.where(mine, tile_code.astype(jnp.float32), 0.0)
            holder = holder + jnp.where(mine, (held // HOLD).astype(jnp.float32), 0.0)
        parts = [to_lanes(code)[:1], to_lanes(holder)[:1], to_lanes(send)[:1]]
        for at, part in enumerate(parts):
            meta_ref[s * 8 + at : s * 8 + at + 1, : part.shape[1]] = part.astype(jnp.int32)
    copy = pltpu.make_async_copy(meta_ref, meta_smem, meta_sem)
    copy.start()
    copy.wait()
    copies = []
    for s in range(STEPS):
        for r in range(N_COL):
            tile = meta_smem[s * 8 + 2, r]
            copies.append(
                pltpu.make_async_copy(tiles_ref.at[s, tile], out_ref.at[r, s], sems.at[len(copies)])
            )
            copies[-1].start()
    for copy in copies:
        copy.wait()


def route(readers, rows, columns, tiles):
    vmem = pl.BlockSpec(memory_space=pltpu.VMEM)
    return pl.pallas_call(
        route_kernel,
        out_shape=(
            jax.ShapeDtypeStruct((8 * STEPS, LANES), jnp.int32),
            jax.ShapeDtypeStruct((N_COL, STEPS, TILE, TILE), jnp.float32),
        ),
        in_specs=[vmem, vmem, vmem, pl.BlockSpec(memory_space=pltpu.HBM)],
        out_specs=(vmem, vmem),
        scratch_shapes=[
            pltpu.SMEM((8 * STEPS, LANES), jnp.int32),
            pltpu.SemaphoreType.DMA,
            pltpu.SemaphoreType.DMA((STEPS * N_COL,)),
        ],
        name="route",
    )(readers, rows, columns, tiles)


def compact_kernel(meta_ref, arrived_ref, amp_ref, side_ref, left_ref, out_ref, minus_ref, plus_ref, sems):
    me_row = lax.axis_index("row")
    copies = []

    def copy(source, target):
        copies.append(pltpu.make_async_copy(source, target, sems.at[len(copies)]))
        copies[-1].start()

    for s in range(STEPS):
        for j in range(CHUNK):
            holder = meta_ref[s * 8 + 1, j * N_ROW + me_row]
            copy(arrived_ref.at[holder, s], out_ref.at[s * CHUNK + j])
    for n, ref in enumerate((amp_ref, side_ref)):
        copy(ref, minus_ref.at[pl.ds(n * STEPS, STEPS)])
    for n, ref in enumerate((left_ref, side_ref)):
        copy(ref, plus_ref.at[pl.ds(n * STEPS, STEPS)])
    for one in copies:
        one.wait()


def compact(meta, arrived, amplitudes, side, amp_left):
    tiles = STEPS * CHUNK
    hbm, vmem = pl.BlockSpec(memory_space=pltpu.HBM), pl.BlockSpec(memory_space=pltpu.VMEM)
    pair = jax.ShapeDtypeStruct((2 * STEPS,) + amplitudes.shape[1:], jnp.float32)
    return pl.pallas_call(
        compact_kernel,
        out_shape=[jax.ShapeDtypeStruct((tiles, TILE, TILE), jnp.float32), pair, pair],
        in_specs=[pl.BlockSpec(memory_space=pltpu.SMEM)] + [hbm] * 4,
        out_specs=[vmem] * 3,
        scratch_shapes=[pltpu.SemaphoreType.DMA((tiles + 4,))],
        compiler_params=pltpu.CompilerParams(vmem_limit_bytes=SMALL_LIMIT),
        name="compact",
    )(meta, arrived, amplitudes, side, amp_left)


def regroup_kernel(plan, *refs):
    outs, sems = refs[-1 - len(plan) : -1], refs[-1]
    copies = []
    for out, parts in zip(outs, plan):
        begin = 0
        for source, first, size in parts:
            copies.append(
                pltpu.make_async_copy(
                    refs[source].at[pl.ds(first, size)], out.at[pl.ds(begin, size)], sems.at[len(copies)]
                )
            )
            copies[-1].start()
            begin += size
    for copy in copies:
        copy.wait()


def regroup(chunks, plan, *earlier):
    any_space = pl.BlockSpec(memory_space=pl.ANY)
    shapes = [
        (sum(size for _, _, size in parts),) + chunks[parts[0][0]].shape[1:] for parts in plan
    ]
    return pl.pallas_call(
        functools.partial(regroup_kernel, plan),
        out_shape=[jax.ShapeDtypeStruct(shape, jnp.float32) for shape in shapes],
        in_specs=[any_space] * (len(chunks) + len(earlier)),
        out_specs=[pl.BlockSpec(memory_space=pltpu.VMEM)] * len(plan),
        scratch_shapes=[pltpu.SemaphoreType.DMA((sum(len(parts) for parts in plan),))],
        compiler_params=pltpu.CompilerParams(vmem_limit_bytes=SMALL_LIMIT),
        name="regroup",
    )(*chunks, *earlier)


def split_kernel(*refs):
    out_ref = refs[-1]
    count = len(refs) // 2
    for core in range(2):
        at = 0
        for ref in refs[core * count : (core + 1) * count]:
            for n in range(ref.shape[0]):
                value = ref[n]
                high = value.astype(jnp.bfloat16)
                out_ref[core, at, :, :TILE] = high
                out_ref[core, at, :, TILE:] = (value - high.astype(jnp.float32)).astype(jnp.bfloat16)
                at += 1


def split_amplitudes(ours, others):
    count, rows = sum(p.shape[0] for p in ours), ours[0].shape[1]
    blocks = [pl.BlockSpec((p.shape[0], rows // 8, TILE), lambda n: (0, n, 0)) for p in ours]
    return pl.pallas_call(
        split_kernel,
        out_shape=jax.ShapeDtypeStruct((2, count, rows, 2 * TILE), jnp.bfloat16),
        grid=(8,),
        in_specs=blocks * 2,
        out_specs=pl.BlockSpec((2, count, rows // 8, 2 * TILE), lambda n: (0, 0, n, 0)),
        compiler_params=pltpu.CompilerParams(vmem_limit_bytes=SMALL_LIMIT),
        cost_estimate=pl.CostEstimate(flops=2**20, bytes_accessed=2**20, transcendentals=0),
        name="split_amplitudes",
    )(*ours, *others)


def product_kernel(places, has_start, meta_ref, *rest):
    chunk_refs = rest[: len(places)]
    amp_ref = rest[len(places)]
    out_ref = rest[-1]
    me_row = lax.axis_index("row")
    me_col = lax.axis_index("col")
    block = out_ref.shape[0] // 2
    if has_start:
        out_ref[...] = rest[len(places) + 1][...]
    else:
        out_ref[...] = jnp.zeros_like(out_ref)
    for ref, runs in zip(chunk_refs, places):
        at = 0
        for dy, dz, first, count in runs:
            source = ((me_row // Z) ^ dy) * Z + (me_row + dz) % Z

            def step(m, ref=ref, source=source, at=at, first=first):
                number = first + m
                s = number // CHUNK
                code = meta_ref[s * 8, (number % CHUNK) * N_ROW + source]
                column = code // NT_DEV
                steps = (column // 4 + 4 - me_col // 4) % 4
                away = (steps ^ (steps // 2)) * 2 + ((column ^ me_col) // 2) % 2
                tile = ref[at + m]
                high = tile.astype(jnp.bfloat16)
                low = (tile - high.astype(jnp.float32)).astype(jnp.bfloat16)
                wide = jnp.concatenate([high, low], axis=1)
                wide = jnp.concatenate([wide, wide], axis=0)
                columns = pl.ds(pl.multiple_of((code % NT_DEV) * TILE, TILE), TILE)
                for begin in range(0, out_ref.shape[0], block):
                    rows = pl.ds(begin, block)
                    both = jnp.dot(
                        amp_ref[(column ^ me_col) % 2, away * STEPS + s, rows],
                        wide,
                        preferred_element_type=jnp.float32,
                    )
                    out_ref[rows, columns] += both[:, :TILE] + both[:, TILE:]

            pl.loop(0, count, unroll=4 if count % 4 == 0 else count)(step)
            at += count


def product(meta, chunks, places, amps, start=None):
    vmem = pl.BlockSpec(memory_space=pltpu.VMEM)
    rows = amps.shape[2]
    operands = list(chunks) + [amps] + ([] if start is None else [start])
    tiles = sum(c.shape[0] for c in chunks)
    return pl.pallas_call(
        functools.partial(product_kernel, places, start is not None),
        out_shape=jax.ShapeDtypeStruct((rows, NT_DEV * TILE), jnp.float32),
        in_specs=[pl.BlockSpec(memory_space=pltpu.SMEM)] + [vmem] * len(operands),
        out_specs=vmem,
        compiler_params=pltpu.CompilerParams(vmem_limit_bytes=VMEM_LIMIT),
        cost_estimate=pl.CostEstimate(
            flops=tiles * rows * TILE, bytes_accessed=2**20, transcendentals=0
        ),
        name="product",
    )(meta, *operands)


def along_z(value, step):
    pairs = [(i, (i // Z) * Z + (i % Z + step) % Z) for i in range(N_ROW)]
    return lax.ppermute(value, "row", pairs)


def across_y(value):
    return lax.ppermute(value, "row", [(i, i ^ Z) for i in range(N_ROW)])


def along_x(value, step):
    pairs = [(c, ((c // 4 + step) % 4) * 4 + c % 4) for c in range(N_COL)]
    return lax.ppermute(value, "col", pairs)


def flip(value, bit):
    return lax.ppermute(value, "col", [(c, c ^ bit) for c in range(N_COL)])


def shards(amplitudes, integrals, tile_rows, tile_reader, tile_column):
    held = (STEPS, tile_rows.shape[1] // LANES, LANES)
    meta, sent = route(
        tile_reader.reshape(held), tile_rows, tile_column, integrals
    )
    side, amp_left = flip(amplitudes, 2), along_x(amplitudes, 1)
    arrived = lax.all_to_all(sent, "col", split_axis=0, concat_axis=0, tiled=True)
    own, minus, plus = compact(meta, arrived, amplitudes, side, amp_left)

    left, right, other = along_z(own, 1), along_z(own, -1), across_y(own)
    from_right, from_left = along_x(minus, -1), along_x(plus, 1)

    up, down, across, side_far, ours = regroup(
        [left, right, other, minus, from_right, from_left, plus],
        [
            [(0, 0, 8), (2, 0, 8)],
            [(1, 8, 8), (2, 8, 8)],
            [(0, 8, 8), (1, 0, 8)],
            [(4, 2, 2)],
            [(3, 0, 4), (4, 0, 4), (6, 0, 2), (5, 2, 2), (5, 0, 2)],
        ],
    )
    up, down, across = along_z(up, 1), along_z(down, -1), across_y(across)
    ours = [ours, along_x(side_far, -1)]
    amps = split_amplitudes(ours, [flip(p, 1) for p in ours])
    places = [[(dy, dz, 0, 16)] for dy, dz in ((0, 0), (0, 3), (0, 1), (1, 0))]
    ladder = product(meta, [own, left, right, other], places, amps)

    far_up, far_down, far_across = regroup([up, down], [[(0, 8, 5)], [(1, 11, 5)], [(0, 5, 3), (1, 0, 3)]], ladder)
    far_up, far_down, far_across = along_z(far_up, 1), along_z(far_down, -1), across_y(far_across)
    places = [
        [(0, 2, 0, 8), (1, 3, 0, 8)],
        [(0, 2, 8, 8), (1, 1, 8, 8)],
        [(1, 3, 8, 8), (1, 1, 0, 8)],
    ]
    ladder = product(meta, [up, down, across], places, amps, ladder)
    places = [[(1, 2, 0, 5)], [(1, 2, 11, 5)], [(1, 2, 5, 6)]]
    return product(meta, [far_up, far_down, far_across], places, amps, ladder)


def solution(mesh):
    return jax.shard_map(
        shards,
        mesh=mesh,
        in_specs=(P(None, "row", "col"), P(None, "col", None, None), P(), P(), P()),
        out_specs=P("row", "col"),
        check_vma=False,
    )
```
